256 devices in a mesh: occ: 32 (over x_lo, z, core), aux: 8 (over y, x_hi).
Axes of the slice: x: 4 (x_hi: 2, x_lo: 2; x = x_hi * 2 + x_lo), y: 4, z: 8, core: 2. Of those that a mesh axis runs over, the one named last changes fastest.
Arguments:
- three_index: bfloat16 [32, 1000, 4096], P('occ', None, 'aux'), may hold values from -0.75 to 0.75
- occ_energy: float32 [32], replicated, may hold values from -2 to -0.5
- vir_energy: float32 [1000], replicated, may hold values from 0.3 to 3
Outputs:
- gamma: float32 [32, 1000, 4096], P('occ', None, 'aux')
The draws below stay inside these ranges and needn't reach their ends.
All inputs are finite; a program needn't handle non-finite values.
Results may differ from the reference program's by a relative error of at most 0.0018.
Values may be sent and summed in bfloat16 or wider, within the bound.
A program may use at most 128 MiB of HBM per device.

```python
import jax
import jax.numpy as jnp
from jax import lax

V = 1000
NAUX = 4096
STEPS = 2
NOCC = 32


def levels(key, shape, split, low, high):
    def one(position, shards_of):
        draws = jax.random.uniform(jax.random.fold_in(jax.random.fold_in(key, 6), position), (shards_of,), jnp.float32, low / len(split), high / len(split))
        return jnp.repeat(jnp.exp(draws), shape[position] // shards_of).reshape((-1,) + (1,) * (len(shape) - position - 1))

    level = one(*split[0])
    for cut in split[1:]:
        level = level * one(*cut)
    return level


def centred(key, extent, scale, most, pieces=(), held_as=jnp.bfloat16):
    gain = levels(key, extent, pieces, -0.22, 0.18) if pieces else 1.0
    entries = jax.random.normal(key, extent, jnp.float32) * scale * gain
    return jnp.minimum(jnp.maximum(entries, -most), most).astype(held_as)


def setup_inputs(seed: int = 0) -> dict:
    splits = jax.random.split(jax.random.key(seed), 4)
    return {
        "three_index": centred(splits[0], (NOCC, V, NAUX), 0.125, 0.75, ((0, 32), (2, 8))),
        "occ_energy": jnp.clip(jax.random.uniform(splits[1], (NOCC,), jnp.float32, -2.0, -0.5), -2.0, -0.5),
        "vir_energy": jnp.clip(jax.random.uniform(splits[2], (V,), jnp.float32, 0.3, 3.0), 0.3, 3.0),
    }


def pair_amplitude(left, right, e_left, e_right, vir_energy):
    summed = jnp.dot(left.astype(jnp.float32), right.astype(jnp.float32).T)
    denom = vir_energy[:, None] + vir_energy[None, :] - e_left - e_right
    return (summed / denom).astype(jnp.bfloat16)


def reference(three_index, occ_energy, vir_energy):
    def one_orbital(index):
        left = three_index[index]
        total = jnp.zeros((V, NAUX), jnp.float32)
        for offset in range(-STEPS, STEPS + 1):
            other = ((index - offset) % NOCC).astype(jnp.int32)
            right = three_index[other]
            amplitude = pair_amplitude(left, right, occ_energy[index], occ_energy[other], vir_energy)
            total = total + jnp.dot(amplitude, right, preferred_element_type=jnp.float32)
        return total

    return lax.map(one_orbital, jnp.arange(NOCC, dtype=jnp.int32))
```

```python
import functools

import jax
import jax.numpy as jnp
from jax import lax
from jax.experimental import pallas as pl
from jax.experimental.pallas import tpu as pltpu
from jax.sharding import PartitionSpec as P

MESH = pl.DeviceIdType.MESH
PAD = 1024
BLOCK = 128
HALF = 512
F32 = jnp.float32
BF16 = jnp.bfloat16


def kernel(
    n_occ, b_ref, occ_ref, vrow_ref, vcol_ref, g_ref,
    nb, kp, kr, am, rsend, rrecv,
    b_ss, b_rs, k_ss, k_rs, a_ss, a_rs, r_ss, r_rs,
):
    occ = lax.axis_index("occ")
    aux = lax.axis_index("aux")
    core = lax.rem(occ, 2)
    y = lax.div(aux, 2)
    h = lax.rem(aux, 2)
    mine = h * 4 + y

    def orbital(d):
        return lax.rem(occ + d + n_occ, n_occ)

    def peer(d):
        dh, dy = d // 4, d % 4
        py, ph = lax.rem(y + dy, 4), lax.rem(h + dh, 2)
        return (occ, py * 2 + ph), ph * 4 + py

    j1 = orbital(-1 - core)
    j2 = orbital(2 - 3 * core)
    to_a = orbital(-2 + 3 * core)
    to_b = orbital(1 + core)
    peers = [peer(d) for d in range(1, 8)]

    barrier = pltpu.get_barrier_semaphore()
    greeted = [dev for dev, _ in peers] + [(j1, aux), (j2, aux), (to_a, aux), (to_b, aux)]
    for dev in greeted:
        pl.semaphore_signal(barrier, inc=1, device_id=dev, device_id_type=MESH)
    pl.semaphore_wait(barrier, len(greeted))

    def remote(src, dst, ss, rs, dev):
        return pltpu.make_async_remote_copy(
            src_ref=src, dst_ref=dst, send_sem=ss, recv_sem=rs, device_id=dev, device_id_type=MESH
        )

    slot = 1 - core
    b_copies = [
        remote(b_ref, nb.at[slot], b_ss.at[n], b_rs.at[slot], (dev, aux))
        for n, dev in enumerate((to_a, to_b))
    ]
    for c in b_copies:
        c.start()

    def rows(block):
        return pl.ds(pl.multiple_of(block * BLOCK, BLOCK), BLOCK)

    def partial_k(k, right):
        @pl.loop(0, 8)
        def _(t):
            r = pl.ds(pl.multiple_of((t // 4) * HALF, HALF), HALF)
            cc = pl.ds(pl.multiple_of((t % 4) * 256, 256), 256)
            part = lax.dot_general(
                b_ref[r, :], right[cc, :], (((1,), (1,)), ((), ())), preferred_element_type=F32
            )
            kp[k, r, cc] = part.astype(BF16)

        copies = []
        for n, (dev, block) in enumerate(peers):
            c = remote(kp.at[k, rows(block)], kr.at[k, rows(mine)], k_ss.at[k, n], k_rs.at[k, mine], dev)
            c.start()
            copies.append(c)
        return copies

    def arrive(k, buf, sems, block, dev):
        remote(buf.at[k, rows(block)], buf.at[k, rows(block)], sems.at[k, block], sems.at[k, block], dev).wait_recv()

    e_mine = occ_ref[occ]

    def amplitude(k, e_other):
        for dev, block in peers:
            arrive(k, kr, k_rs, block, dev)

        @pl.loop(0, 8)
        def _(t):
            lo = t * 16
            total = kp[k, pl.ds(pl.multiple_of(mine * BLOCK + lo, 16), 16), :].astype(F32)
            for _, block in peers:
                total += kr[k, pl.ds(pl.multiple_of(block * BLOCK + lo, 16), 16), :].astype(F32)
            va = vcol_ref[pl.ds(pl.multiple_of(mine * BLOCK + lo, 16), 16), :]
            denom = va + vrow_ref[...] - e_mine - e_other
            am[k, pl.ds(pl.multiple_of(mine * BLOCK + lo, 16), 16), :] = (total / denom).astype(BF16)

        copies = []
        for n, (dev, block) in enumerate(peers):
            c = remote(am.at[k, rows(mine)], am.at[k, rows(mine)], a_ss.at[k, n], a_rs.at[k, mine], dev)
            c.start()
            copies.append(c)
        return copies

    def gather(k):
        for dev, block in peers:
            arrive(k, am, a_rs, block, dev)

    def add_gamma(k, right, first):
        @pl.loop(0, 4)
        def _(t):
            r = pl.ds(pl.multiple_of((t // 2) * HALF, HALF), HALF)
            cc = pl.ds(pl.multiple_of((t % 2) * 256, 256), 256)
            term = jnp.dot(am[k, r, :], right[:, cc], preferred_element_type=F32)
            if first:
                g_ref[r, cc] = term
            else:
                g_ref[r, cc] += term

    def give_back(k, n, dev):
        @pl.loop(0, 4)
        def _(t):
            r = pl.ds(pl.multiple_of((t // 2) * HALF, HALF), HALF)
            cc = pl.ds(pl.multiple_of((t % 2) * 256, 256), 256)
            term = lax.dot_general(
                am[k, :, r], b_ref[:, cc], (((0,), (0,)), ((), ())), preferred_element_type=F32
            )
            rsend[n, r, cc] = term.astype(BF16)

        c = remote(rsend.at[n], rrecv.at[core], r_ss.at[n], r_rs.at[core], (dev, aux))
        c.start()
        return c

    sent = []
    sent += partial_k(0, b_ref)
    remote(b_ref, nb.at[1], b_ss.at[1], b_rs.at[1], (j2, aux)).wait_recv()
    sent += partial_k(2, nb.at[1])
    remote(b_ref, nb.at[0], b_ss.at[0], b_rs.at[0], (j1, aux)).wait_recv()
    sent += partial_k(1, nb.at[0])
    sent += amplitude(0, e_mine)
    sent += amplitude(2, occ_ref[j2])
    sent += amplitude(1, occ_ref[j1])
    gather(0)
    add_gamma(0, b_ref, True)
    gather(2)
    r2 = give_back(2, 1, j2)
    add_gamma(2, nb.at[1], False)
    gather(1)
    r1 = give_back(1, 0, j1)
    add_gamma(1, nb.at[0], False)
    for c in b_copies:
        c.wait_send()
    for c in sent:
        c.wait_send()
    r2.wait_send()
    r1.wait_send()
    for n in range(2):
        remote(rsend.at[n], rrecv.at[n], r_ss.at[n], r_rs.at[n], (to_a, aux)).wait_recv()

    @pl.loop(0, 8)
    def _(t):
        r = pl.ds(pl.multiple_of(t * BLOCK, BLOCK), BLOCK)
        g_ref[r, :] += rrecv[0, r, :].astype(F32) + rrecv[1, r, :].astype(F32)


def local(n_occ, three_index, occ_energy, vir_energy):
    v = three_index.shape[1]
    b = jnp.pad(three_index[0], ((0, PAD - v), (0, 0)))
    vir = jnp.pad(vir_energy, (0, PAD - v), constant_values=1.0)
    width = b.shape[1]
    vmem = pl.BlockSpec(memory_space=pltpu.VMEM)
    dma = pltpu.SemaphoreType.DMA
    gamma = pl.pallas_call(
        functools.partial(kernel, n_occ),
        out_shape=jax.ShapeDtypeStruct((PAD, width), F32),
        in_specs=[vmem, pl.BlockSpec(memory_space=pltpu.SMEM), vmem, vmem],
        out_specs=vmem,
        scratch_shapes=[
            pltpu.VMEM((2, PAD, width), BF16),
            pltpu.VMEM((3, PAD, PAD), BF16),
            pltpu.VMEM((3, PAD, PAD), BF16),
            pltpu.VMEM((3, PAD, PAD), BF16),
            pltpu.VMEM((2, PAD, width), BF16),
            pltpu.VMEM((2, PAD, width), BF16),
            dma((2,)), dma((2,)),
            dma((3, 7)), dma((3, 8)),
            dma((3, 7)), dma((3, 8)),
            dma((2,)), dma((2,)),
        ],
        compiler_params=pltpu.CompilerParams(
            collective_id=0, has_side_effects=True, vmem_limit_bytes=56 * 2**20
        ),
        cost_estimate=pl.CostEstimate(flops=8 * 10**9, bytes_accessed=4 * 10**6, transcendentals=0),
    )(b, occ_energy, vir[None, :], vir[:, None])
    return gamma[None, :v]


def solution(mesh):
    placed = (P("occ", None, "aux"), P(), P())
    return jax.shard_map(
        functools.partial(local, mesh.shape["occ"]),
        mesh=mesh, in_specs=placed, out_specs=P("occ", None, "aux"), check_vma=False,
    )
```

```python
import functools

import jax
import jax.numpy as jnp
from jax import lax
from jax.experimental import pallas as pl
from jax.experimental.pallas import tpu as pltpu
from jax.sharding import PartitionSpec as P

MESH = pl.DeviceIdType.MESH
PAD = 1024
BLOCK = 128
HALF = 512
SPLIT = 512
F32 = jnp.float32
BF16 = jnp.bfloat16


def kernel(
    n_occ, b_ref, occ_ref, vrow_ref, vcol_ref, g_ref,
    bp, nbo, nbp, kf, kp, kr, am, ret, rchip, rz,
    x_ss, x_rs, z_ss, z_rs, c_ss, c_rs, k_ss, k_rs, a_ss, a_rs, r_ss, r_rs,
):
    occ = lax.axis_index("occ")
    aux = lax.axis_index("aux")
    core = lax.rem(occ, 2)
    y = lax.div(aux, 2)
    h = lax.rem(aux, 2)
    o = 1 - h
    yp, ym, yy = lax.rem(y + 1, 4), lax.rem(y + 3, 4), lax.rem(y + 2, 4)

    def orbital(d):
        return lax.rem(occ + d + n_occ, n_occ)

    across = (occ, y * 2 + o)
    up, down, far = [(occ, q * 2 + h) for q in (yp, ym, yy)]
    sibling = (occ + 1 - 2 * core, aux)
    z_out = (orbital(4 * core - 2), aux)
    z_in = (orbital(2 - 4 * core), aux)
    zs, cs = 1 - core, core
    e_mine = occ_ref[occ]
    e_pair = (e_mine, occ_ref[orbital(-1 - core)], occ_ref[orbital(2 - 3 * core)])

    barrier = pltpu.get_barrier_semaphore()
    greeted = (across, up, down, far, sibling, z_out, z_in)
    for dev in greeted:
        pl.semaphore_signal(barrier, inc=1, device_id=dev, device_id_type=MESH)
    pl.semaphore_wait(barrier, len(greeted))

    def remote(src, dst, ss, rs, dev):
        return pltpu.make_async_remote_copy(
            src_ref=src, dst_ref=dst, send_sem=ss, recv_sem=rs, device_id=dev, device_id_type=MESH
        )

    sent = []

    def push(*args):
        c = remote(*args)
        c.start()
        sent.append(c)

    def ds(start, size):
        return pl.ds(pl.multiple_of(start, size), size)

    rows_h, rows_o = ds(h * HALF, HALF), ds(o * HALF, HALF)

    push(b_ref.at[rows_o, :], bp.at[rows_o, :], x_ss.at[0], x_rs.at[0], across)
    push(b_ref.at[rows_h, :], bp.at[rows_h, :], x_ss.at[1], x_rs.at[1], across)

    def b_part(n, source):
        if source is None:
            return (b_ref.at[rows_h, :], bp.at[rows_h, :], b_ref.at[rows_o, :])[n]
        return (nbo.at[source, rows_h, :], nbp.at[source], nbo.at[source, rows_o, :])[n]

    def z_send(n):
        push(b_part(n, None), b_part(n, zs), z_ss.at[n], z_rs.at[n], z_out)

    def chip_send(n, source):
        remote(b_part(n, source), b_part(n, 1 - core), c_ss.at[n], c_rs.at[n], sibling).start()

    def z_arrive(n):
        remote(b_part(n, zs), b_part(n, zs), z_ss.at[n], z_rs.at[n], z_in).wait_recv()

    def chip_arrive(n):
        remote(b_part(n, cs), b_part(n, cs), c_ss.at[n], c_rs.at[n], sibling).wait_recv()

    def own_to_chip(n):
        @pl.when(core == 0)
        def _():
            chip_send(n, None)

    def slot_to_chip(n):
        z_arrive(n)

        @pl.when(core == 1)
        def _():
            chip_send(n, 0)

    def partial_k(k, ab):
        c = o if ab else h
        cols = ds(c * HALF, HALF)
        left, left_p = (b_ref[rows_h, :], bp[rows_h, :]) if k == 0 else (nbo[k - 1, rows_h, :], nbp[k - 1])
        contract = (((1,), (1,)), ((), ()))
        part = lax.dot_general(left, b_ref[cols, :], contract, preferred_element_type=F32)
        part += lax.dot_general(left_p, bp[cols, :], contract, preferred_element_type=F32)
        kf[k, :, cols] = part
        kp[k, :, cols] = part.astype(BF16)
        for n, (q, dev) in enumerate(((yp, up), (ym, down), (yy, far))):
            push(
                kp.at[k, ds(q * BLOCK, BLOCK), cols], kr.at[k, ds(y * BLOCK, BLOCK), cols],
                k_ss.at[k, ab, n], k_rs.at[k, ab, y], dev,
            )

    base = h * HALF + y * BLOCK

    def amplitude(k):
        for ab in range(2):
            cols = ds((o if ab else h) * HALF, HALF)
            for q, dev in ((yp, up), (ym, down), (yy, far)):
                ref = kr.at[k, ds(q * BLOCK, BLOCK), cols]
                remote(ref, ref, k_rs.at[k, ab, q], k_rs.at[k, ab, q], dev).wait_recv()

        @pl.loop(0, 4)
        def _(t):
            total = kf[k, ds(y * BLOCK + t * 32, 32), :]
            for q in (yp, ym, yy):
                total += kr[k, ds(q * BLOCK + t * 32, 32), :].astype(F32)
            mine = ds(base + t * 32, 32)
            denom = vcol_ref[mine, :] + vrow_ref[...] - e_mine - e_pair[k]
            am[k, mine, :] = (total / denom).astype(BF16)

    first_cols, last_cols = pl.ds(0, SPLIT), pl.ds(SPLIT, PAD - SPLIT)
    all_cols = pl.ds(0, PAD)

    def piece(k, n):
        q, low = ((ym, 0), (yp, 0), (yy, 0), (yy, 64), (y, 0), (ym, 0), (yp, 0), (yy, 0), (yy, 64), (ym, 0), (yp, 0), (yy, 0))[n]
        side = h if n < 4 else o
        count = 64 if n in (2, 3, 7, 8) else BLOCK
        cols = all_cols if n < 5 else first_cols if n < 9 else last_cols
        return am.at[k, ds(side * HALF + q * BLOCK + low, count), cols]

    def gather_from(k, n):
        dev = (down, up, down, up, across, down, up, down, up, across, across, across)[n]
        remote(piece(k, n), piece(k, n), a_ss.at[k, n], a_rs.at[k, n], dev).wait_recv()

    def spread(k, n, side, q, low, count, cols, dev):
        ref = am.at[k, ds(side * HALF + q * BLOCK + low, count), cols]
        push(ref, ref, a_ss.at[k, n], a_rs.at[k, n], dev)

    def stage1(k):
        spread(k, 4, h, y, 0, BLOCK, all_cols, across)
        spread(k, 0, h, y, 0, BLOCK, all_cols, up)
        spread(k, 1, h, y, 0, BLOCK, all_cols, down)

    def stage2(k):
        gather_from(k, 0)
        spread(k, 2, h, ym, 0, 64, all_cols, up)
        spread(k, 9, h, ym, 0, BLOCK, last_cols, across)
        gather_from(k, 1)
        spread(k, 3, h, yp, 64, 64, all_cols, down)
        spread(k, 10, h, yp, 0, BLOCK, last_cols, across)
        gather_from(k, 4)
        spread(k, 5, o, y, 0, BLOCK, first_cols, up)
        spread(k, 6, o, y, 0, BLOCK, first_cols, down)

    def stage3(k):
        gather_from(k, 2)
        gather_from(k, 3)
        spread(k, 11, h, yy, 0, BLOCK, last_cols, across)
        gather_from(k, 5)
        spread(k, 7, o, ym, 0, 64, first_cols, up)
        gather_from(k, 6)
        spread(k, 8, o, yp, 64, 64, first_cols, down)

    def stage4(k):
        for n in (7, 8, 9, 10, 11):
            gather_from(k, n)

    def product(k, transposed, right, store):
        @pl.loop(0, 2)
        def _(t):
            r = ds(t * HALF, HALF)
            if transposed:
                term = lax.dot_general(am[k, :, r], right, (((0,), (0,)), ((), ())), preferred_element_type=F32)
            else:
                term = jnp.dot(am[k, r, :], right, preferred_element_type=F32)
            store(r, term)

    def set_gamma(r, term):
        g_ref[r, :] = term

    def add_gamma(r, term):
        g_ref[r, :] += term

    def set_return(n):
        def store(r, term):
            ret[n, r, :] = term.astype(BF16)

        return store

    z_send(0)
    own_to_chip(0)
    slot_to_chip(0)
    remote(bp.at[rows_h, :], bp.at[rows_h, :], x_ss.at[0], x_rs.at[0], across).wait_recv()
    z_send(1)
    own_to_chip(1)
    partial_k(0, 0)
    z_send(2)
    own_to_chip(2)
    slot_to_chip(1)
    chip_arrive(0)
    chip_arrive(1)
    partial_k(2, 0)
    partial_k(1, 0)
    remote(bp.at[rows_o, :], bp.at[rows_o, :], x_ss.at[1], x_rs.at[1], across).wait_recv()
    partial_k(1, 1)
    partial_k(2, 1)
    partial_k(0, 1)
    slot_to_chip(2)
    amplitude(1)
    stage1(1)
    amplitude(2)
    stage1(2)
    stage2(1)
    amplitude(0)
    stage1(0)
    stage2(2)
    stage3(1)
    stage2(0)
    stage3(2)
    chip_arrive(2)

    def return_to(n, dev, dst, m):
        return remote(ret.at[n], dst, r_ss.at[m], r_rs.at[m], dev)

    stage4(1)
    product(1, False, b_ref[...], set_return(0))

    @pl.when(core == 0)
    def _():
        return_to(0, sibling, rchip, 0).start()

    product(1, True, nbo[0], set_gamma)

    @pl.when(core == 1)
    def _():
        return_to(0, sibling, rchip, 0).wait_recv()

        @pl.loop(0, 8)
        def _(t):
            r = ds(t * BLOCK, BLOCK)
            ret[0, r, :] = (ret[0, r, :].astype(F32) + rchip[r, :].astype(F32)).astype(BF16)

        return_to(0, z_in, rz, 1).start()

    stage3(0)
    stage4(2)
    product(2, False, b_ref[...], set_return(1))

    @pl.when(core == 0)
    def _():
        return_to(1, z_in, rz, 1).start()

    @pl.when(core == 1)
    def _():
        return_to(1, sibling, rchip, 0).start()

    product(2, True, nbo[1], add_gamma)
    stage4(0)
    product(0, False, b_ref[...], add_gamma)
    return_to(1, z_out, rz, 1).wait_recv()

    @pl.loop(0, 8)
    def _(t):
        r = ds(t * BLOCK, BLOCK)
        g_ref[r, :] += rz[r, :].astype(F32)

    @pl.when(core == 0)
    def _():
        return_to(1, sibling, rchip, 0).wait_recv()

        @pl.loop(0, 8)
        def _(t):
            r = ds(t * BLOCK, BLOCK)
            g_ref[r, :] += rchip[r, :].astype(F32)

    for c in sent:
        c.wait_send()
    for n in range(3):
        remote(b_part(n, cs), b_part(n, cs), c_ss.at[n], c_rs.at[n], sibling).wait_send()
    for m in range(2):
        return_to(0, sibling, rchip, m).wait_send()


def local(n_occ, three_index, occ_energy, vir_energy):
    v = three_index.shape[1]
    b = jnp.pad(three_index[0], ((0, PAD - v), (0, 0)))
    vir = jnp.pad(vir_energy, (0, PAD - v), constant_values=1.0)
    width = b.shape[1]
    vmem = pl.BlockSpec(memory_space=pltpu.VMEM)
    dma = pltpu.SemaphoreType.DMA
    gamma = pl.pallas_call(
        functools.partial(kernel, n_occ),
        out_shape=jax.ShapeDtypeStruct((PAD, width), F32),
        in_specs=[vmem, pl.BlockSpec(memory_space=pltpu.SMEM), vmem, vmem],
        out_specs=vmem,
        scratch_shapes=[
            pltpu.VMEM((PAD, width), BF16),
            pltpu.VMEM((2, PAD, width), BF16),
            pltpu.VMEM((2, HALF, width), BF16),
            pltpu.VMEM((3, HALF, PAD), F32),
            pltpu.VMEM((3, HALF, PAD), BF16),
            pltpu.VMEM((3, HALF, PAD), BF16),
            pltpu.VMEM((3, PAD, PAD), BF16),
            pltpu.VMEM((2, PAD, width), BF16),
            pltpu.VMEM((PAD, width), BF16),
            pltpu.VMEM((PAD, width), BF16),
            dma((2,)), dma((2,)),
            dma((3,)), dma((3,)),
            dma((3,)), dma((3,)),
            dma((3, 2, 3)), dma((3, 2, 4)),
            dma((3, 12)), dma((3, 12)),
            dma((2,)), dma((2,)),
        ],
        compiler_params=pltpu.CompilerParams(
            collective_id=0, has_side_effects=True, vmem_limit_bytes=56 * 2**20
        ),
        cost_estimate=pl.CostEstimate(flops=8 * 10**9, bytes_accessed=4 * 10**6, transcendentals=0),
    )(b, occ_energy, vir[None, :], vir[:, None])
    return gamma[None, :v]


def solution(mesh):
    placed = (P("occ", None, "aux"), P(), P())
    return jax.shard_map(
        functools.partial(local, mesh.shape["occ"]),
        mesh=mesh, in_specs=placed, out_specs=P("occ", None, "aux"), check_vma=False,
    )
```

```python
import functools

import jax
import jax.numpy as jnp
from jax import lax
from jax.experimental import pallas as pl
from jax.experimental.pallas import tpu as pltpu
from jax.sharding import PartitionSpec as P

MESH = pl.DeviceIdType.MESH
PAD = 1024
BLOCK = 128
HALF = 512
SPLITS = (512, 640)
SPLITS_SELF = (384, 512)
SELF_COLS = 768
F32 = jnp.float32
BF16 = jnp.bfloat16


def kernel(
    n_occ, b_in, occ_ref, vir_ref, g_ref,
    b_ref, vrow, vcol, bp, nbo, nbp, kf, kp, kr, am, ret, rchip, rz,
    x_ss, x_rs, z_ss, z_rs, c_ss, c_rs, k_ss, k_rs, a_ss, a_rs, r_ss, r_rs,
):
    occ = lax.axis_index("occ")
    aux = lax.axis_index("aux")
    core = lax.rem(occ, 2)
    y = lax.div(aux, 2)
    h = lax.rem(aux, 2)
    o = 1 - h
    z = lax.rem(lax.div(occ, 2), 8)
    crowded = z * (7 - z) == 0
    yp, ym, yy = lax.rem(y + 1, 4), lax.rem(y + 3, 4), lax.rem(y + 2, 4)

    def orbital(d):
        return lax.rem(occ + d + n_occ, n_occ)

    across = (occ, y * 2 + o)
    up, down, far = [(occ, q * 2 + h) for q in (yp, ym, yy)]
    sibling = (occ + 1 - 2 * core, aux)
    z_out = (orbital(4 * core - 2), aux)
    z_in = (orbital(2 - 4 * core), aux)
    zs, cs = 1 - core, core
    e_mine = occ_ref[occ]
    e_pair = (e_mine, occ_ref[orbital(-1 - core)], occ_ref[orbital(2 - 3 * core)])

    barrier = pltpu.get_barrier_semaphore()
    greeted = (across, up, down, far, sibling, z_out, z_in)
    for dev in greeted:
        pl.semaphore_signal(barrier, inc=1, device_id=dev, device_id_type=MESH)

    v = b_in.shape[0]
    whole = v // 16 * 16
    b_ref[:whole, :] = b_in[:whole, :]
    tail = jnp.zeros((PAD - v, b_in.shape[1]), F32)
    b_ref[whole:, :] = jnp.concatenate([b_in[whole:, :].astype(F32), tail], axis=0).astype(BF16)
    vrow[...] = jnp.ones_like(vrow)
    vrow[:, :v] = vir_ref[...]
    base = pl.multiple_of(h * HALF + y * BLOCK, BLOCK)
    here = jnp.broadcast_to(vrow[:, pl.ds(base, BLOCK)], (BLOCK, BLOCK))
    diagonal = lax.broadcasted_iota(jnp.int32, (BLOCK, BLOCK), 0) == lax.broadcasted_iota(jnp.int32, (BLOCK, BLOCK), 1)
    vcol[...] = jnp.sum(jnp.where(diagonal, here, 0.0), axis=1, keepdims=True)
    pl.semaphore_wait(barrier, len(greeted))

    def remote(src, dst, ss, rs, dev):
        return pltpu.make_async_remote_copy(
            src_ref=src, dst_ref=dst, send_sem=ss, recv_sem=rs, device_id=dev, device_id_type=MESH
        )

    sent = []

    def push(*args):
        c = remote(*args)
        c.start()
        sent.append(c)

    def ds(start, size):
        return pl.ds(pl.multiple_of(start, size), size)

    rows_h, rows_o = ds(h * HALF, HALF), ds(o * HALF, HALF)

    push(b_ref.at[rows_o, :], bp.at[rows_o, :], x_ss.at[0], x_rs.at[0], across)

    def b_part(n, source):
        if source is None:
            return (b_ref.at[rows_h, :], bp.at[rows_h, :], b_ref.at[rows_o, :])[n]
        return (nbo.at[source, rows_h, :], nbp.at[source], nbo.at[source, rows_o, :])[n]

    def z_send(n):
        push(b_part(n, None), b_part(n, zs), z_ss.at[n], z_rs.at[n], z_out)

    def chip_send(n, source):
        remote(b_part(n, source), b_part(n, 1 - core), c_ss.at[n], c_rs.at[n], sibling).start()

    def z_arrive(n):
        remote(b_part(n, zs), b_part(n, zs), z_ss.at[n], z_rs.at[n], z_in).wait_recv()

    def chip_arrive(n):
        remote(b_part(n, cs), b_part(n, cs), c_ss.at[n], c_rs.at[n], sibling).wait_recv()

    def own_to_chip(n):
        @pl.when(core == 0)
        def _():
            chip_send(n, None)

    def slot_to_chip(n):
        z_arrive(n)

        @pl.when(core == 1)
        def _():
            chip_send(n, 0)

    def k_cols(k, ab):
        if k == 0:
            return pl.ds(HALF, 256) if ab else pl.ds(0, HALF)
        return ds((o if ab else h) * HALF, HALF)

    contract = (((1,), (1,)), ((), ()))

    def partial_k(k, ab):
        cols = k_cols(k, ab)
        if k == 0 and ab:
            for s in range(2):
                left = ds(h * HALF + s * 256, 256)
                right = ds(o * HALF + lax.rem(s + h, 2) * 256, 256)
                part = lax.dot_general(b_ref[left, :], b_ref[right, :], contract, preferred_element_type=F32)
                part += lax.dot_general(bp[left, :], bp[right, :], contract, preferred_element_type=F32)
                kf[k, pl.ds(s * 256, 256), cols] = part
                kp[k, pl.ds(s * 256, 256), cols] = part.astype(BF16)
        else:
            right = ds((o if ab else h) * HALF, HALF)
            left, left_p = (b_ref[rows_h, :], bp[rows_h, :]) if k == 0 else (nbo[k - 1, rows_h, :], nbp[k - 1])
            part = lax.dot_general(left, b_ref[right, :], contract, preferred_element_type=F32)
            part += lax.dot_general(left_p, bp[right, :], contract, preferred_element_type=F32)
            kf[k, :, cols] = part
            kp[k, :, cols] = part.astype(BF16)
        for n, (q, dev) in enumerate(((yp, up), (ym, down), (yy, far))):
            push(
                kp.at[k, ds(q * BLOCK, BLOCK), cols], kr.at[k, ds(y * BLOCK, BLOCK), cols],
                k_ss.at[k, ab, n], k_rs.at[k, ab, y], dev,
            )

    def amplitude(k):
        for ab in range(2):
            cols = k_cols(k, ab)
            for q, dev in ((yp, up), (ym, down), (yy, far)):
                ref = kr.at[k, ds(q * BLOCK, BLOCK), cols]
                remote(ref, ref, k_rs.at[k, ab, q], k_rs.at[k, ab, q], dev).wait_recv()
            energy = cols
            if k == 0:
                energy = ds(o * HALF + lax.rem(y // 2 + h, 2) * 256, 256) if ab else rows_h

            @pl.loop(0, 4)
            def _(t):
                total = kf[k, ds(y * BLOCK + t * 32, 32), cols]
                for q in (yp, ym, yy):
                    total += kr[k, ds(q * BLOCK + t * 32, 32), cols].astype(F32)
                denom = vcol[ds(t * 32, 32), :] + vrow[:, energy] - e_mine - e_pair[k]
                am[k, ds(base + t * 32, 32), cols] = (total / denom).astype(BF16)

    def piece(k, n, side, q, low, w):
        count = 64 if n in (2, 3, 7, 8) else BLOCK
        width = PAD if k else SELF_COLS
        split = (SPLITS if k else SPLITS_SELF)[w]
        cols = pl.ds(0, width) if n < 5 else pl.ds(0, split) if n < 9 else pl.ds(split, width - split)
        return am.at[k, ds(side * HALF + q * BLOCK + low, count), cols]

    def by_plane(f):
        pl.when(crowded)(lambda: f(1))
        pl.when(jnp.logical_not(crowded))(lambda: f(0))

    def spread(k, n, side, q, low, dev, w=0):
        ref = piece(k, n, side, q, low, w)
        remote(ref, ref, a_ss.at[k, n], a_rs.at[k, n], dev).start()

    def gather_from(k, n, w=0):
        q, low = ((ym, 0), (yp, 0), (yy, 0), (yy, 64), (y, 0), (ym, 0), (yp, 0), (yy, 0), (yy, 64), (ym, 0), (yp, 0), (yy, 0))[n]
        dev = (down, up, down, up, across, down, up, down, up, across, across, across)[n]
        ref = piece(k, n, h if n < 4 else o, q, low, w)
        remote(ref, ref, a_ss.at[k, n], a_rs.at[k, n], dev).wait_recv()

    def stage1(k):
        spread(k, 4, h, y, 0, across)
        spread(k, 0, h, y, 0, up)
        spread(k, 1, h, y, 0, down)

    def stage2(k):
        @by_plane
        def _(w):
            gather_from(k, 0)
            spread(k, 2, h, ym, 0, up)
            spread(k, 9, h, ym, 0, across, w)
            gather_from(k, 1)
            spread(k, 3, h, yp, 64, down)
            spread(k, 10, h, yp, 0, across, w)
            gather_from(k, 4)
            spread(k, 5, o, y, 0, up, w)
            spread(k, 6, o, y, 0, down, w)

    def stage3(k):
        @by_plane
        def _(w):
            gather_from(k, 2)
            gather_from(k, 3)
            spread(k, 11, h, yy, 0, across, w)
            gather_from(k, 5, w)
            spread(k, 7, o, ym, 0, up, w)
            gather_from(k, 6, w)
            spread(k, 8, o, yp, 64, down, w)

    def stage4(k):
        @by_plane
        def _(w):
            for n in (7, 8, 9, 10, 11):
                gather_from(k, n, w)

    def product(k, transposed, right, store):
        @pl.loop(0, 2)
        def _(t):
            r = ds(t * HALF, HALF)
            if transposed:
                term = lax.dot_general(am[k, :, r], right, (((0,), (0,)), ((), ())), preferred_element_type=F32)
            else:
                term = jnp.dot(am[k, r, :], right, preferred_element_type=F32)
            store(r, term)

    def set_gamma(r, term):
        g_ref[r, :] = term

    def add_gamma(r, term):
        g_ref[r, :] += term

    def set_return(n):
        def store(r, term):
            ret[n, r, :] = term.astype(BF16)

        return store

    def self_product():
        for side in range(2):
            r = pl.ds(side * HALF, HALF)
            g_ref[r, :] += jnp.dot(am[0, r, pl.ds(0, HALF)], b_ref[r, :], preferred_element_type=F32)
        for side in range(2):
            for s in range(2):
                r = pl.ds(side * HALF + s * 256, 256)
                c = pl.ds((1 - side) * HALF + (s + side) % 2 * 256, 256)
                block = am[0, r, pl.ds(HALF, 256)]
                g_ref[r, :] += jnp.dot(block, b_ref[c, :], preferred_element_type=F32)
                g_ref[c, :] += lax.dot_general(block, b_ref[r, :], (((0,), (0,)), ((), ())), preferred_element_type=F32)

    def return_part(n, half, dst, dev):
        rows = rows_o if half else rows_h
        m = 0 if dst is rchip else 1
        return remote(ret.at[n, rows, :], dst.at[rows, :], r_ss.at[m, half], r_rs.at[m, half], dev)

    def give_back(k, half):
        rows = rows_o if half else rows_h
        ret[k - 1, rows, :] = jnp.dot(am[k, rows, :], b_ref[...], preferred_element_type=F32).astype(BF16)

        @pl.when(core == k - 1)
        def _():
            return_part(k - 1, half, rchip, sibling).start()

        if k == 2:
            @pl.when(core == 0)
            def _():
                return_part(1, half, rz, z_in).start()

    def merge(half):
        rows = rows_o if half else rows_h

        @pl.when(core == 1)
        def _():
            return_part(0, half, rchip, sibling).wait_recv()
            ret[0, rows, :] = (ret[0, rows, :].astype(F32) + rchip[rows, :].astype(F32)).astype(BF16)
            return_part(0, half, rz, z_in).start()

    z_send(0)
    own_to_chip(0)
    slot_to_chip(0)
    remote(bp.at[rows_h, :], bp.at[rows_h, :], x_ss.at[0], x_rs.at[0], across).wait_recv()
    z_send(1)
    own_to_chip(1)
    push(b_ref.at[rows_h, :], bp.at[rows_h, :], x_ss.at[1], x_rs.at[1], across)
    partial_k(0, 0)
    slot_to_chip(1)
    chip_arrive(0)
    chip_arrive(1)
    partial_k(2, 0)
    partial_k(1, 0)
    remote(bp.at[rows_o, :], bp.at[rows_o, :], x_ss.at[1], x_rs.at[1], across).wait_recv()
    z_send(2)
    own_to_chip(2)
    partial_k(1, 1)
    partial_k(2, 1)
    partial_k(0, 1)
    amplitude(1)
    stage1(1)
    slot_to_chip(2)
    amplitude(2)
    stage1(2)
    stage2(1)
    amplitude(0)
    stage1(0)
    stage2(2)
    stage3(1)
    give_back(1, 0)
    merge(0)
    stage3(2)
    give_back(2, 0)
    stage2(0)
    chip_arrive(2)
    stage4(1)
    give_back(1, 1)
    product(1, True, nbo[0], set_gamma)
    merge(1)
    stage3(0)
    stage4(2)
    give_back(2, 1)
    product(2, True, nbo[1], add_gamma)
    stage4(0)
    self_product()
    for half in range(2):
        return_part(1, half, rz, z_out).wait_recv()

    @pl.loop(0, 8)
    def _(t):
        r = ds(t * BLOCK, BLOCK)
        g_ref[r, :] += rz[r, :].astype(F32)

    @pl.when(core == 0)
    def _():
        for half in range(2):
            return_part(1, half, rchip, sibling).wait_recv()

        @pl.loop(0, 8)
        def _(t):
            r = ds(t * BLOCK, BLOCK)
            g_ref[r, :] += rchip[r, :].astype(F32)

    for c in sent:
        c.wait_send()

    @by_plane
    def _(w):
        for k in range(3):
            for n in range(12):
                ref = piece(k, n, 0, 0, 0, w)
                remote(ref, ref, a_ss.at[k, n], a_rs.at[k, n], across).wait_send()

    for n in range(3):
        remote(b_part(n, cs), b_part(n, cs), c_ss.at[n], c_rs.at[n], sibling).wait_send()
    for half in range(2):
        return_part(0, half, rchip, sibling).wait_send()
        return_part(0, half, rz, z_in).wait_send()


def local(n_occ, three_index, occ_energy, vir_energy):
    v = three_index.shape[1]
    width = three_index.shape[2]
    vmem = pl.BlockSpec(memory_space=pltpu.VMEM)
    dma = pltpu.SemaphoreType.DMA
    gamma = pl.pallas_call(
        functools.partial(kernel, n_occ),
        out_shape=jax.ShapeDtypeStruct((PAD, width), F32),
        in_specs=[vmem, pl.BlockSpec(memory_space=pltpu.SMEM), vmem],
        out_specs=vmem,
        scratch_shapes=[
            pltpu.VMEM((PAD, width), BF16),
            pltpu.VMEM((1, PAD), F32),
            pltpu.VMEM((BLOCK, 1), F32),
            pltpu.VMEM((PAD, width), BF16),
            pltpu.VMEM((2, PAD, width), BF16),
            pltpu.VMEM((2, HALF, width), BF16),
            pltpu.VMEM((3, HALF, PAD), F32),
            pltpu.VMEM((3, HALF, PAD), BF16),
            pltpu.VMEM((3, HALF, PAD), BF16),
            pltpu.VMEM((3, PAD, PAD), BF16),
            pltpu.VMEM((2, PAD, width), BF16),
            pltpu.VMEM((PAD, width), BF16),
            pltpu.VMEM((PAD, width), BF16),
            dma((2,)), dma((2,)),
            dma((3,)), dma((3,)),
            dma((3,)), dma((3,)),
            dma((3, 2, 3)), dma((3, 2, 4)),
            dma((3, 12)), dma((3, 12)),
            dma((2, 2)), dma((2, 2)),
        ],
        compiler_params=pltpu.CompilerParams(
            collective_id=0, has_side_effects=True, vmem_limit_bytes=56 * 2**20
        ),
        cost_estimate=pl.CostEstimate(flops=8 * 10**9, bytes_accessed=4 * 10**6, transcendentals=0),
    )(three_index[0], occ_energy, vir_energy[None, :])
    return gamma[None, :v]


def solution(mesh):
    placed = (P("occ", None, "aux"), P(), P())
    return jax.shard_map(
        functools.partial(local, mesh.shape["occ"]),
        mesh=mesh, in_specs=placed, out_specs=P("occ", None, "aux"), check_vma=False,
    )
```

```python
import functools

import jax
import jax.numpy as jnp
from jax import lax
from jax.experimental import pallas as pl
from jax.experimental.pallas import tpu as pltpu
from jax.sharding import PartitionSpec as P

MESH = pl.DeviceIdType.MESH
PAD = 1024
BLOCK = 128
HALF = 512
SPLITS = ((640, 640), (384, 512), (512, 640))
SELF_COLS = 768
F32 = jnp.float32
BF16 = jnp.bfloat16


def kernel(
    n_occ, b_in, occ_ref, vir_ref, g_ref,
    b_ref, vrow, vcol, bp, nbo, nbp, kf, kp, kr, kx, km, am, ret, rchip, rz,
    x_ss, x_rs, z_ss, z_rs, c_ss, c_rs, k_ss, k_rs, a_ss, a_rs, r_ss, r_rs,
):
    occ = lax.axis_index("occ")
    aux = lax.axis_index("aux")
    core = lax.rem(occ, 2)
    y = lax.div(aux, 2)
    h = lax.rem(aux, 2)
    o = 1 - h
    z = lax.rem(lax.div(occ, 2), 8)
    crowded = z * (7 - z) == 0
    yp, ym, yy = lax.rem(y + 1, 4), lax.rem(y + 3, 4), lax.rem(y + 2, 4)

    def orbital(d):
        return lax.rem(occ + d + n_occ, n_occ)

    across = (occ, y * 2 + o)
    up, down, far = [(occ, q * 2 + h) for q in (yp, ym, yy)]
    sibling = (occ + 1 - 2 * core, aux)
    z_out = (orbital(4 * core - 2), aux)
    z_in = (orbital(2 - 4 * core), aux)
    zs, cs = 1 - core, core
    e_mine = occ_ref[occ]
    e_pair = (e_mine, occ_ref[orbital(-1 - core)], occ_ref[orbital(2 - 3 * core)])

    barrier = pltpu.get_barrier_semaphore()
    greeted = (across, up, down, far, sibling, z_out, z_in)
    for dev in greeted:
        pl.semaphore_signal(barrier, inc=1, device_id=dev, device_id_type=MESH)

    v = b_in.shape[0]
    whole = v // 16 * 16
    b_ref[:whole, :] = b_in[:whole, :]
    tail = jnp.zeros((PAD - v, b_in.shape[1]), F32)
    b_ref[whole:, :] = jnp.concatenate([b_in[whole:, :].astype(F32), tail], axis=0).astype(BF16)
    vrow[...] = jnp.ones_like(vrow)
    vrow[:, :v] = vir_ref[...]
    base = pl.multiple_of(h * HALF + y * BLOCK, BLOCK)
    here = jnp.broadcast_to(vrow[:, pl.ds(base, BLOCK)], (BLOCK, BLOCK))
    diagonal = lax.broadcasted_iota(jnp.int32, (BLOCK, BLOCK), 0) == lax.broadcasted_iota(jnp.int32, (BLOCK, BLOCK), 1)
    vcol[...] = jnp.sum(jnp.where(diagonal, here, 0.0), axis=1, keepdims=True)
    pl.semaphore_wait(barrier, len(greeted))

    def remote(src, dst, ss, rs, dev):
        return pltpu.make_async_remote_copy(
            src_ref=src, dst_ref=dst, send_sem=ss, recv_sem=rs, device_id=dev, device_id_type=MESH
        )

    sent = []

    def push(*args):
        c = remote(*args)
        c.start()
        sent.append(c)

    def ds(start, size):
        return pl.ds(pl.multiple_of(start, size), size)

    rows_h, rows_o = ds(h * HALF, HALF), ds(o * HALF, HALF)

    push(b_ref.at[rows_o, :], bp.at[rows_o, :], x_ss.at[0], x_rs.at[0], across)

    def b_part(n, source):
        if source is None:
            return (b_ref.at[rows_h, :], bp.at[rows_h, :], b_ref.at[rows_o, :])[n]
        return (nbo.at[source, rows_h, :], nbp.at[source], nbo.at[source, rows_o, :])[n]

    def z_send(n):
        push(b_part(n, None), b_part(n, zs), z_ss.at[n], z_rs.at[n], z_out)

    def chip_send(n, source):
        remote(b_part(n, source), b_part(n, 1 - core), c_ss.at[n], c_rs.at[n], sibling).start()

    def z_arrive(n):
        remote(b_part(n, zs), b_part(n, zs), z_ss.at[n], z_rs.at[n], z_in).wait_recv()

    def chip_arrive(n):
        remote(b_part(n, cs), b_part(n, cs), c_ss.at[n], c_rs.at[n], sibling).wait_recv()

    def own_to_chip(n):
        @pl.when(core == 0)
        def _():
            chip_send(n, None)

    def slot_to_chip(n):
        z_arrive(n)

        @pl.when(core == 1)
        def _():
            chip_send(n, 0)

    def k_cols(k, ab, part=None):
        start, size = (HALF if ab else 0, 256 if ab else HALF) if k == 0 else ((o if ab else h) * HALF, HALF)
        if part is not None:
            size //= 2
            start = start + part * size
        return ds(start, size)

    contract = (((1,), (1,)), ((), ()))

    def partial_k(k, ab):
        cols = k_cols(k, ab)
        if k == 0 and ab:
            for s in range(2):
                left = ds(h * HALF + s * 256, 256)
                right = ds(o * HALF + lax.rem(s + h, 2) * 256, 256)
                part = lax.dot_general(b_ref[left, :], b_ref[right, :], contract, preferred_element_type=F32)
                part += lax.dot_general(bp[left, :], bp[right, :], contract, preferred_element_type=F32)
                kf[k, pl.ds(s * 256, 256), cols] = part
                kp[k, pl.ds(s * 256, 256), cols] = part.astype(BF16)
        else:
            right = ds((o if ab else h) * HALF, HALF)
            left, left_p = (b_ref[rows_h, :], bp[rows_h, :]) if k == 0 else (nbo[k - 1, rows_h, :], nbp[k - 1])
            part = lax.dot_general(left, b_ref[right, :], contract, preferred_element_type=F32)
            part += lax.dot_general(left_p, bp[right, :], contract, preferred_element_type=F32)
            kf[k, :, cols] = part
            kp[k, :, cols] = part.astype(BF16)
        push(kp.at[k, ds(yy * BLOCK, BLOCK), k_cols(k, ab, 0)], relayed(k, ab, 0), k_ss.at[k, ab, 0], k_rs.at[k, ab, 0], up)
        push(kp.at[k, ds(yy * BLOCK, BLOCK), k_cols(k, ab, 1)], relayed(k, ab, 1), k_ss.at[k, ab, 1], k_rs.at[k, ab, 1], down)
        push(kp.at[k, ds(yp * BLOCK, BLOCK), k_cols(k, ab, 1)], arrived(k, ab, 0, 1), k_ss.at[k, ab, 2], k_rs.at[k, ab, 2], up)
        push(kp.at[k, ds(ym * BLOCK, BLOCK), k_cols(k, ab, 0)], arrived(k, ab, 1, 0), k_ss.at[k, ab, 3], k_rs.at[k, ab, 3], down)

    def half_cols(k, ab):
        return pl.ds(0, 128 if k == 0 and ab else 256)

    def relayed(k, ab, way):
        return kx.at[k, ab, way, :, half_cols(k, ab)]

    def arrived(k, ab, way, part):
        return kr.at[k, way, :, k_cols(k, ab, part)]

    def pass_on(k, ab):
        for way, (source, target, q) in enumerate(((down, up, yp), (up, down, ym))):
            ref = relayed(k, ab, way)
            remote(ref, ref, k_rs.at[k, ab, way], k_rs.at[k, ab, way], source).wait_recv()
            width = half_cols(k, ab)
            own = kf[k, ds(q * BLOCK, BLOCK), k_cols(k, ab, way)]
            km[k, ab, way, :, width] = (own + kx[k, ab, way, :, width].astype(F32)).astype(BF16)
            push(
                km.at[k, ab, way, :, width], arrived(k, ab, way, way),
                k_ss.at[k, ab, 4 + way], k_rs.at[k, ab, 4 + way], target,
            )

    def amplitude(k):
        for ab in range(2):
            cols = k_cols(k, ab)
            for n, (way, part) in ((2, (0, 1)), (3, (1, 0)), (4, (0, 0)), (5, (1, 1))):
                ref = arrived(k, ab, way, part)
                remote(ref, ref, k_rs.at[k, ab, n], k_rs.at[k, ab, n], up if way else down).wait_recv()
            energy = cols
            if k == 0:
                energy = ds(o * HALF + lax.rem(y // 2 + h, 2) * 256, 256) if ab else rows_h

            @pl.loop(0, 4)
            def _(t):
                total = kf[k, ds(y * BLOCK + t * 32, 32), cols]
                for way in range(2):
                    total += kr[k, way, ds(t * 32, 32), cols].astype(F32)
                denom = vcol[ds(t * 32, 32), :] + vrow[:, energy] - e_mine - e_pair[k]
                am[k, ds(base + t * 32, 32), cols] = (total / denom).astype(BF16)

    def piece(k, n, side, q, low, w):
        count = 64 if n in (2, 3, 7, 8) else BLOCK
        width = PAD if k else SELF_COLS
        split = SPLITS[k][w]
        cols = pl.ds(0, width) if n < 5 else pl.ds(0, split) if n < 9 else pl.ds(split, width - split)
        return am.at[k, ds(side * HALF + q * BLOCK + low, count), cols]

    def by_plane(f):
        pl.when(crowded)(lambda: f(1))
        pl.when(jnp.logical_not(crowded))(lambda: f(0))

    def spread(k, n, side, q, low, dev, w=0):
        ref = piece(k, n, side, q, low, w)
        remote(ref, ref, a_ss.at[k, n], a_rs.at[k, n], dev).start()

    def gather_from(k, n, w=0):
        q, low = ((ym, 0), (yp, 0), (yy, 0), (yy, 64), (y, 0), (ym, 0), (yp, 0), (yy, 0), (yy, 64), (ym, 0), (yp, 0), (yy, 0))[n]
        dev = (down, up, down, up, across, down, up, down, up, across, across, across)[n]
        ref = piece(k, n, h if n < 4 else o, q, low, w)
        remote(ref, ref, a_ss.at[k, n], a_rs.at[k, n], dev).wait_recv()

    def stage1(k):
        spread(k, 4, h, y, 0, across)
        spread(k, 0, h, y, 0, up)
        spread(k, 1, h, y, 0, down)

    def stage2(k):
        @by_plane
        def _(w):
            gather_from(k, 0)
            spread(k, 2, h, ym, 0, up)
            spread(k, 9, h, ym, 0, across, w)
            gather_from(k, 1)
            spread(k, 3, h, yp, 64, down)
            spread(k, 10, h, yp, 0, across, w)
            gather_from(k, 4)
            spread(k, 5, o, y, 0, up, w)
            spread(k, 6, o, y, 0, down, w)

    def stage3(k):
        @by_plane
        def _(w):
            gather_from(k, 2)
            gather_from(k, 3)
            spread(k, 11, h, yy, 0, across, w)
            gather_from(k, 5, w)
            spread(k, 7, o, ym, 0, up, w)
            gather_from(k, 6, w)
            spread(k, 8, o, yp, 64, down, w)

    def stage4(k):
        @by_plane
        def _(w):
            for n in (7, 8, 9, 10, 11):
                gather_from(k, n, w)

    def product(k, transposed, right, store):
        @pl.loop(0, 2)
        def _(t):
            r = ds(t * HALF, HALF)
            if transposed:
                term = lax.dot_general(am[k, :, r], right, (((0,), (0,)), ((), ())), preferred_element_type=F32)
            else:
                term = jnp.dot(am[k, r, :], right, preferred_element_type=F32)
            store(r, term)

    def set_gamma(r, term):
        g_ref[r, :] = term

    def add_gamma(r, term):
        g_ref[r, :] += term

    def set_return(n):
        def store(r, term):
            ret[n, r, :] = term.astype(BF16)

        return store

    def self_product():
        for side in range(2):
            r = pl.ds(side * HALF, HALF)
            g_ref[r, :] += jnp.dot(am[0, r, pl.ds(0, HALF)], b_ref[r, :], preferred_element_type=F32)
        for side in range(2):
            for s in range(2):
                r = pl.ds(side * HALF + s * 256, 256)
                c = pl.ds((1 - side) * HALF + (s + side) % 2 * 256, 256)
                block = am[0, r, pl.ds(HALF, 256)]
                g_ref[r, :] += jnp.dot(block, b_ref[c, :], preferred_element_type=F32)
                g_ref[c, :] += lax.dot_general(block, b_ref[r, :], (((0,), (0,)), ((), ())), preferred_element_type=F32)

    def return_part(n, half, dst, dev):
        rows = rows_o if half else rows_h
        m = 0 if dst is rchip else 1
        return remote(ret.at[n, rows, :], dst.at[rows, :], r_ss.at[m, half], r_rs.at[m, half], dev)

    def give_back(k, half):
        rows = rows_o if half else rows_h
        ret[k - 1, rows, :] = jnp.dot(am[k, rows, :], b_ref[...], preferred_element_type=F32).astype(BF16)

        @pl.when(core == k - 1)
        def _():
            return_part(k - 1, half, rchip, sibling).start()

        if k == 2:
            @pl.when(core == 0)
            def _():
                return_part(1, half, rz, z_in).start()

    def merge(half):
        rows = rows_o if half else rows_h

        @pl.when(core == 1)
        def _():
            return_part(0, half, rchip, sibling).wait_recv()
            ret[0, rows, :] = (ret[0, rows, :].astype(F32) + rchip[rows, :].astype(F32)).astype(BF16)
            return_part(0, half, rz, z_in).start()

    z_send(0)
    push(b_ref.at[rows_h, :], bp.at[rows_h, :], x_ss.at[1], x_rs.at[1], across)
    own_to_chip(0)
    slot_to_chip(0)
    remote(bp.at[rows_h, :], bp.at[rows_h, :], x_ss.at[0], x_rs.at[0], across).wait_recv()
    z_send(1)
    own_to_chip(1)
    partial_k(0, 0)
    slot_to_chip(1)
    chip_arrive(0)
    chip_arrive(1)
    partial_k(2, 0)
    pass_on(0, 0)
    partial_k(1, 0)
    pass_on(2, 0)
    remote(bp.at[rows_o, :], bp.at[rows_o, :], x_ss.at[1], x_rs.at[1], across).wait_recv()
    z_send(2)
    own_to_chip(2)
    partial_k(1, 1)
    pass_on(1, 0)
    partial_k(2, 1)
    pass_on(1, 1)
    partial_k(0, 1)
    pass_on(2, 1)
    amplitude(1)
    stage1(1)
    pass_on(0, 1)
    slot_to_chip(2)
    amplitude(2)
    stage1(2)
    stage2(1)
    amplitude(0)
    stage1(0)
    stage2(2)
    stage3(1)
    give_back(1, 0)
    merge(0)
    stage3(2)
    give_back(2, 0)
    stage2(0)
    chip_arrive(2)
    stage4(1)
    give_back(1, 1)
    product(1, True, nbo[0], set_gamma)
    merge(1)
    stage3(0)
    stage4(2)
    give_back(2, 1)
    product(2, True, nbo[1], add_gamma)
    stage4(0)
    self_product()
    for half in range(2):
        return_part(1, half, rz, z_out).wait_recv()

    @pl.loop(0, 8)
    def _(t):
        r = ds(t * BLOCK, BLOCK)
        g_ref[r, :] += rz[r, :].astype(F32)

    @pl.when(core == 0)
    def _():
        for half in range(2):
            return_part(1, half, rchip, sibling).wait_recv()

        @pl.loop(0, 8)
        def _(t):
            r = ds(t * BLOCK, BLOCK)
            g_ref[r, :] += rchip[r, :].astype(F32)

    for c in sent:
        c.wait_send()

    @by_plane
    def _(w):
        for k in range(3):
            for n in range(12):
                ref = piece(k, n, 0, 0, 0, w)
                remote(ref, ref, a_ss.at[k, n], a_rs.at[k, n], across).wait_send()

    for n in range(3):
        remote(b_part(n, cs), b_part(n, cs), c_ss.at[n], c_rs.at[n], sibling).wait_send()
    for half in range(2):
        return_part(0, half, rchip, sibling).wait_send()
        return_part(0, half, rz, z_in).wait_send()


def local(n_occ, three_index, occ_energy, vir_energy):
    v = three_index.shape[1]
    width = three_index.shape[2]
    vmem = pl.BlockSpec(memory_space=pltpu.VMEM)
    dma = pltpu.SemaphoreType.DMA
    gamma = pl.pallas_call(
        functools.partial(kernel, n_occ),
        out_shape=jax.ShapeDtypeStruct((PAD, width), F32),
        in_specs=[vmem, pl.BlockSpec(memory_space=pltpu.SMEM), vmem],
        out_specs=vmem,
        scratch_shapes=[
            pltpu.VMEM((PAD, width), BF16),
            pltpu.VMEM((1, PAD), F32),
            pltpu.VMEM((BLOCK, 1), F32),
            pltpu.VMEM((PAD, width), BF16),
            pltpu.VMEM((2, PAD, width), BF16),
            pltpu.VMEM((2, HALF, width), BF16),
            pltpu.VMEM((3, HALF, PAD), F32),
            pltpu.VMEM((3, HALF, PAD), BF16),
            pltpu.VMEM((3, 2, BLOCK, PAD), BF16),
            pltpu.VMEM((3, 2, 2, BLOCK, 256), BF16),
            pltpu.VMEM((3, 2, 2, BLOCK, 256), BF16),
            pltpu.VMEM((3, PAD, PAD), BF16),
            pltpu.VMEM((2, PAD, width), BF16),
            pltpu.VMEM((PAD, width), BF16),
            pltpu.VMEM((PAD, width), BF16),
            dma((2,)), dma((2,)),
            dma((3,)), dma((3,)),
            dma((3,)), dma((3,)),
            dma((3, 2, 6)), dma((3, 2, 6)),
            dma((3, 12)), dma((3, 12)),
            dma((2, 2)), dma((2, 2)),
        ],
        compiler_params=pltpu.CompilerParams(
            collective_id=0, has_side_effects=True, vmem_limit_bytes=56 * 2**20
        ),
        cost_estimate=pl.CostEstimate(flops=8 * 10**9, bytes_accessed=4 * 10**6, transcendentals=0),
    )(three_index[0], occ_energy, vir_energy[None, :])
    return gamma[None, :v]


def solution(mesh):
    placed = (P("occ", None, "aux"), P(), P())
    return jax.shard_map(
        functools.partial(local, mesh.shape["occ"]),
        mesh=mesh, in_specs=placed, out_specs=P("occ", None, "aux"), check_vma=False,
    )
```

```python
import functools

import jax
import jax.numpy as jnp
from jax import lax
from jax.experimental import pallas as pl
from jax.experimental.pallas import tpu as pltpu
from jax.sharding import PartitionSpec as P

MESH = pl.DeviceIdType.MESH
PAD = 1024
BLOCK = 128
HALF = 512
SPLITS = ((512, 512), (512, 512), (512, 640))
SELF_COLS = 640
SELF_NEAR = 384
F32 = jnp.float32
BF16 = jnp.bfloat16


def kernel(
    n_occ, b_in, occ_ref, vir_ref, g_ref,
    b_ref, vrow, vwrap, quad, vcol, bp, nbo, nbp, kf, kp, kr, kx, km, am, ret, rchip, rz,
    x_ss, x_rs, z_ss, z_rs, c_ss, c_rs, k_ss, k_rs, a_ss, a_rs, r_ss, r_rs,
):
    occ = lax.axis_index("occ")
    aux = lax.axis_index("aux")
    core = lax.rem(occ, 2)
    y = lax.div(aux, 2)
    h = lax.rem(aux, 2)
    o = 1 - h
    z = lax.rem(lax.div(occ, 2), 8)
    crowded = z * (7 - z) == 0
    yp, ym, yy = lax.rem(y + 1, 4), lax.rem(y + 3, 4), lax.rem(y + 2, 4)

    def orbital(d):
        return lax.rem(occ + d + n_occ, n_occ)

    across = (occ, y * 2 + o)
    up, down, far = [(occ, q * 2 + h) for q in (yp, ym, yy)]
    sibling = (occ + 1 - 2 * core, aux)
    z_out = (orbital(4 * core - 2), aux)
    z_in = (orbital(2 - 4 * core), aux)
    zs, cs = 1 - core, core
    e_mine = occ_ref[occ]
    e_pair = (e_mine, occ_ref[orbital(-1 - core)], occ_ref[orbital(2 - 3 * core)])

    barrier = pltpu.get_barrier_semaphore()
    greeted = (across, up, down, far, sibling, z_out, z_in)
    for dev in greeted:
        pl.semaphore_signal(barrier, inc=1, device_id=dev, device_id_type=MESH)

    v = b_in.shape[0]
    whole = v // 16 * 16
    b_ref[:whole, :] = b_in[:whole, :]
    tail = jnp.zeros((PAD - v, b_in.shape[1]), F32)
    b_ref[whole:, :] = jnp.concatenate([b_in[whole:, :].astype(F32), tail], axis=0).astype(BF16)
    vrow[...] = jnp.ones_like(vrow)
    vrow[:, :v] = vir_ref[...]
    for n in range(2):
        vwrap[:, n * HALF:(n + 1) * HALF] = vrow[:, pl.ds(pl.multiple_of(h * HALF, HALF), HALF)]
    base = pl.multiple_of(h * HALF + y * BLOCK, BLOCK)
    here = jnp.broadcast_to(vrow[:, pl.ds(base, BLOCK)], (BLOCK, BLOCK))
    diagonal = lax.broadcasted_iota(jnp.int32, (BLOCK, BLOCK), 0) == lax.broadcasted_iota(jnp.int32, (BLOCK, BLOCK), 1)
    vcol[...] = jnp.sum(jnp.where(diagonal, here, 0.0), axis=1, keepdims=True)
    pl.semaphore_wait(barrier, len(greeted))

    def remote(src, dst, ss, rs, dev):
        return pltpu.make_async_remote_copy(
            src_ref=src, dst_ref=dst, send_sem=ss, recv_sem=rs, device_id=dev, device_id_type=MESH
        )

    sent = []

    def push(*args):
        c = remote(*args)
        c.start()
        sent.append(c)

    def ds(start, size):
        return pl.ds(pl.multiple_of(start, size), size)

    rows_h, rows_o = ds(h * HALF, HALF), ds(o * HALF, HALF)

    push(b_ref.at[rows_o, :], bp.at[rows_o, :], x_ss.at[0], x_rs.at[0], across)

    def b_part(n, source):
        if source is None:
            return (b_ref.at[rows_h, :], bp.at[rows_h, :], b_ref.at[rows_o, :])[n]
        return (nbo.at[source, rows_h, :], nbp.at[source], nbo.at[source, rows_o, :])[n]

    def z_send(n):
        push(b_part(n, None), b_part(n, zs), z_ss.at[n], z_rs.at[n], z_out)

    def chip_send(n, source):
        remote(b_part(n, source), b_part(n, 1 - core), c_ss.at[n], c_rs.at[n], sibling).start()

    def z_arrive(n):
        remote(b_part(n, zs), b_part(n, zs), z_ss.at[n], z_rs.at[n], z_in).wait_recv()

    def chip_arrive(n):
        remote(b_part(n, cs), b_part(n, cs), c_ss.at[n], c_rs.at[n], sibling).wait_recv()

    def own_to_chip(n):
        @pl.when(core == 0)
        def _():
            chip_send(n, None)

    def slot_to_chip(n):
        z_arrive(n)

        @pl.when(core == 1)
        def _():
            chip_send(n, 0)

    def k_cols(k, ab):
        if k == 0:
            return pl.ds(SELF_NEAR, 256) if ab else pl.ds(0, SELF_NEAR)
        return ds((o if ab else h) * HALF, HALF)

    def half_rows(q, part):
        return ds(q * BLOCK + part * 64, 64)

    contract = (((1,), (1,)), ((), ()))

    def partial_k(k, ab):
        cols = k_cols(k, ab)
        if k == 0 and ab:
            for s in range(2):
                left = ds(h * HALF + s * 256, 256)
                right = ds(o * HALF + lax.rem(s + h, 2) * 256, 256)
                part = lax.dot_general(b_ref[left, :], b_ref[right, :], contract, preferred_element_type=F32)
                part += lax.dot_general(bp[left, :], bp[right, :], contract, preferred_element_type=F32)
                kf[k, pl.ds(s * 256, 256), cols] = part
                kp[k, pl.ds(s * 256, 256), cols] = part.astype(BF16)
        else:
            right = ds((o if ab else h) * HALF, HALF)
            left, left_p = (b_ref[rows_h, :], bp[rows_h, :]) if k == 0 else (nbo[k - 1, rows_h, :], nbp[k - 1])
            part = lax.dot_general(left, b_ref[right, :], contract, preferred_element_type=F32)
            part += lax.dot_general(left_p, bp[right, :], contract, preferred_element_type=F32)
            if k:
                kf[k, :, cols] = part
                kp[k, :, cols] = part.astype(BF16)
            else:
                for q in range(4):
                    for d in range(3):
                        r, c, at = q * BLOCK, (q + d) % 4 * BLOCK, d * BLOCK
                        block = part[r:r + BLOCK, c:c + BLOCK]
                        kf[0, r:r + BLOCK, at:at + BLOCK] = block
                        kp[0, r:r + BLOCK, at:at + BLOCK] = block.astype(BF16)
        push(kp.at[k, half_rows(yy, 0), cols], relayed(k, ab, 0), k_ss.at[k, ab, 0], k_rs.at[k, ab, 0], up)
        push(kp.at[k, half_rows(yy, 1), cols], relayed(k, ab, 1), k_ss.at[k, ab, 1], k_rs.at[k, ab, 1], down)
        push(kp.at[k, half_rows(yp, 1), cols], arrived(k, ab, 0, 1), k_ss.at[k, ab, 2], k_rs.at[k, ab, 2], up)
        push(kp.at[k, half_rows(ym, 0), cols], arrived(k, ab, 1, 0), k_ss.at[k, ab, 3], k_rs.at[k, ab, 3], down)

    def run(k, ab):
        return pl.ds(0, HALF if k else 256 if ab else SELF_NEAR)

    def relayed(k, ab, way):
        return kx.at[k, ab, way, :, run(k, ab)]

    def arrived(k, ab, way, part):
        return kr.at[k, way, pl.ds(part * 64, 64), k_cols(k, ab)]

    def pass_on(k, ab):
        for way, (source, target, q) in enumerate(((down, up, yp), (up, down, ym))):
            ref = relayed(k, ab, way)
            remote(ref, ref, k_rs.at[k, ab, way], k_rs.at[k, ab, way], source).wait_recv()
            width = run(k, ab)
            own = kf[k, half_rows(q, way), k_cols(k, ab)]
            km[k, ab, way, :, width] = (own + kx[k, ab, way, :, width].astype(F32)).astype(BF16)
            push(
                km.at[k, ab, way, :, width], arrived(k, ab, way, way),
                k_ss.at[k, ab, 4 + way], k_rs.at[k, ab, 4 + way], target,
            )

    def amplitude(k):
        for ab in range(2):
            cols = k_cols(k, ab)
            for n, (way, part) in ((2, (0, 1)), (3, (1, 0)), (4, (0, 0)), (5, (1, 1))):
                ref = arrived(k, ab, way, part)
                remote(ref, ref, k_rs.at[k, ab, n], k_rs.at[k, ab, n], up if way else down).wait_recv()
            source, energy = vrow, cols
            if k == 0 and ab:
                energy = ds(o * HALF + lax.rem(y // 2 + h, 2) * 256, 256)
            elif k == 0:
                source, energy = vwrap, pl.ds(pl.multiple_of(y * BLOCK, BLOCK), SELF_NEAR)

            @pl.loop(0, 4)
            def _(t):
                total = kf[k, ds(y * BLOCK + t * 32, 32), cols]
                for way in range(2):
                    total += kr[k, way, ds(t * 32, 32), cols].astype(F32)
                denom = vcol[ds(t * 32, 32), :] + source[:, energy] - e_mine - e_pair[k]
                am[k, ds(base + t * 32, 32), cols] = (total / denom).astype(BF16)

    def piece(k, n, side, q, low, w):
        count = 64 if n in (2, 3, 7, 8) else BLOCK
        width = PAD if k else SELF_COLS
        split = SPLITS[k][w]
        cols = pl.ds(0, width) if n < 5 else pl.ds(0, split) if n < 9 else pl.ds(split, width - split)
        return am.at[k, ds(side * HALF + q * BLOCK + low, count), cols]

    def by_plane(f):
        pl.when(crowded)(lambda: f(1))
        pl.when(jnp.logical_not(crowded))(lambda: f(0))

    def spread(k, n, side, q, low, dev, w=0):
        ref = piece(k, n, side, q, low, w)
        remote(ref, ref, a_ss.at[k, n], a_rs.at[k, n], dev).start()

    def gather_from(k, n, w=0):
        q, low = ((ym, 0), (yp, 0), (yy, 0), (yy, 64), (y, 0), (ym, 0), (yp, 0), (yy, 0), (yy, 64), (ym, 0), (yp, 0), (yy, 0))[n]
        dev = (down, up, down, up, across, down, up, down, up, across, across, across)[n]
        ref = piece(k, n, h if n < 4 else o, q, low, w)
        remote(ref, ref, a_ss.at[k, n], a_rs.at[k, n], dev).wait_recv()

    def stage1(k):
        spread(k, 4, h, y, 0, across)
        spread(k, 0, h, y, 0, up)
        spread(k, 1, h, y, 0, down)

    def stage2(k):
        @by_plane
        def _(w):
            gather_from(k, 0)
            spread(k, 2, h, ym, 0, up)
            spread(k, 9, h, ym, 0, across, w)
            gather_from(k, 1)
            spread(k, 3, h, yp, 64, down)
            spread(k, 10, h, yp, 0, across, w)
            gather_from(k, 4)
            spread(k, 5, o, y, 0, up, w)
            spread(k, 6, o, y, 0, down, w)

    def stage3(k):
        @by_plane
        def _(w):
            gather_from(k, 2)
            gather_from(k, 3)
            spread(k, 11, h, yy, 0, across, w)
            gather_from(k, 5, w)
            spread(k, 7, o, ym, 0, up, w)
            gather_from(k, 6, w)
            spread(k, 8, o, yp, 64, down, w)

    def stage4(k):
        @by_plane
        def _(w):
            for n in (7, 8, 9, 10, 11):
                gather_from(k, n, w)

    def product(k, transposed, right, store):
        @pl.loop(0, 2)
        def _(t):
            r = ds(t * HALF, HALF)
            if transposed:
                term = lax.dot_general(am[k, :, r], right, (((0,), (0,)), ((), ())), preferred_element_type=F32)
            else:
                term = jnp.dot(am[k, r, :], right, preferred_element_type=F32)
            store(r, term)

    def set_gamma(r, term):
        g_ref[r, :] = term

    def add_gamma(r, term):
        g_ref[r, :] += term

    def set_return(n):
        def store(r, term):
            ret[n, r, :] = term.astype(BF16)

        return store

    def self_product():
        for side in range(2):
            for q in range(4):
                r, last = q * BLOCK, (q + 3) % 4 * BLOCK
                for d in range(3):
                    c = (q + d) % 4 * BLOCK
                    quad[r:r + BLOCK, c:c + BLOCK] = am[0, pl.ds(side * HALF + r, BLOCK), pl.ds(d * BLOCK, BLOCK)]
                quad[r:r + BLOCK, last:last + BLOCK] = am[0, pl.ds(side * HALF + last, BLOCK), pl.ds(BLOCK, BLOCK)].T
            r = pl.ds(side * HALF, HALF)
            g_ref[r, :] += jnp.dot(quad[...], b_ref[r, :], preferred_element_type=F32)
        for side in range(2):
            for s in range(2):
                r = pl.ds(side * HALF + s * 256, 256)
                c = pl.ds((1 - side) * HALF + (s + side) % 2 * 256, 256)
                block = am[0, r, pl.ds(SELF_NEAR, 256)]
                g_ref[r, :] += jnp.dot(block, b_ref[c, :], preferred_element_type=F32)
                g_ref[c, :] += lax.dot_general(block, b_ref[r, :], (((0,), (0,)), ((), ())), preferred_element_type=F32)

    def return_part(n, half, dst, dev):
        rows = rows_o if half else rows_h
        m = 0 if dst is rchip else 1
        return remote(ret.at[n, rows, :], dst.at[rows, :], r_ss.at[m, half], r_rs.at[m, half], dev)

    def give_back(k, half):
        rows = rows_o if half else rows_h
        ret[k - 1, rows, :] = jnp.dot(am[k, rows, :], b_ref[...], preferred_element_type=F32).astype(BF16)

        @pl.when(core == k - 1)
        def _():
            return_part(k - 1, half, rchip, sibling).start()

        if k == 2:
            @pl.when(core == 0)
            def _():
                return_part(1, half, rz, z_in).start()

    def merge(half):
        rows = rows_o if half else rows_h

        @pl.when(core == 1)
        def _():
            return_part(0, half, rchip, sibling).wait_recv()
            ret[0, rows, :] = (ret[0, rows, :].astype(F32) + rchip[rows, :].astype(F32)).astype(BF16)
            return_part(0, half, rz, z_in).start()

    z_send(0)
    push(b_ref.at[rows_h, :], bp.at[rows_h, :], x_ss.at[1], x_rs.at[1], across)
    own_to_chip(0)
    slot_to_chip(0)
    remote(bp.at[rows_h, :], bp.at[rows_h, :], x_ss.at[0], x_rs.at[0], across).wait_recv()
    z_send(1)
    own_to_chip(1)
    partial_k(0, 0)
    slot_to_chip(1)
    chip_arrive(0)
    chip_arrive(1)
    partial_k(2, 0)
    pass_on(0, 0)
    partial_k(1, 0)
    pass_on(2, 0)
    remote(bp.at[rows_o, :], bp.at[rows_o, :], x_ss.at[1], x_rs.at[1], across).wait_recv()
    z_send(2)
    own_to_chip(2)
    partial_k(1, 1)
    pass_on(1, 0)
    partial_k(2, 1)
    pass_on(1, 1)
    partial_k(0, 1)
    pass_on(2, 1)
    amplitude(1)
    stage1(1)
    pass_on(0, 1)
    slot_to_chip(2)
    amplitude(2)
    stage1(2)
    stage2(1)
    amplitude(0)
    stage1(0)
    stage2(2)
    stage3(1)
    give_back(1, 0)
    merge(0)
    stage3(2)
    give_back(2, 0)
    stage2(0)
    chip_arrive(2)
    stage4(1)
    give_back(1, 1)
    product(1, True, nbo[0], set_gamma)
    merge(1)
    stage3(0)
    stage4(2)
    give_back(2, 1)
    product(2, True, nbo[1], add_gamma)
    stage4(0)
    self_product()
    for half in range(2):
        return_part(1, half, rz, z_out).wait_recv()

    @pl.loop(0, 8)
    def _(t):
        r = ds(t * BLOCK, BLOCK)
        g_ref[r, :] += rz[r, :].astype(F32)

    @pl.when(core == 0)
    def _():
        for half in range(2):
            return_part(1, half, rchip, sibling).wait_recv()

        @pl.loop(0, 8)
        def _(t):
            r = ds(t * BLOCK, BLOCK)
            g_ref[r, :] += rchip[r, :].astype(F32)

    for c in sent:
        c.wait_send()

    @by_plane
    def _(w):
        for k in range(3):
            for n in range(12):
                ref = piece(k, n, 0, 0, 0, w)
                remote(ref, ref, a_ss.at[k, n], a_rs.at[k, n], across).wait_send()

    for n in range(3):
        remote(b_part(n, cs), b_part(n, cs), c_ss.at[n], c_rs.at[n], sibling).wait_send()
    for half in range(2):
        return_part(0, half, rchip, sibling).wait_send()
        return_part(0, half, rz, z_in).wait_send()


def local(n_occ, three_index, occ_energy, vir_energy):
    v = three_index.shape[1]
    width = three_index.shape[2]
    vmem = pl.BlockSpec(memory_space=pltpu.VMEM)
    dma = pltpu.SemaphoreType.DMA
    gamma = pl.pallas_call(
        functools.partial(kernel, n_occ),
        out_shape=jax.ShapeDtypeStruct((PAD, width), F32),
        in_specs=[vmem, pl.BlockSpec(memory_space=pltpu.SMEM), vmem],
        out_specs=vmem,
        scratch_shapes=[
            pltpu.VMEM((PAD, width), BF16),
            pltpu.VMEM((1, PAD), F32),
            pltpu.VMEM((1, PAD), F32),
            pltpu.VMEM((HALF, HALF), BF16),
            pltpu.VMEM((BLOCK, 1), F32),
            pltpu.VMEM((PAD, width), BF16),
            pltpu.VMEM((2, PAD, width), BF16),
            pltpu.VMEM((2, HALF, width), BF16),
            pltpu.VMEM((3, HALF, PAD), F32),
            pltpu.VMEM((3, HALF, PAD), BF16),
            pltpu.VMEM((3, 2, BLOCK, PAD), BF16),
            pltpu.VMEM((3, 2, 2, 64, HALF), BF16),
            pltpu.VMEM((3, 2, 2, 64, HALF), BF16),
            pltpu.VMEM((3, PAD, PAD), BF16),
            pltpu.VMEM((2, PAD, width), BF16),
            pltpu.VMEM((PAD, width), BF16),
            pltpu.VMEM((PAD, width), BF16),
            dma((2,)), dma((2,)),
            dma((3,)), dma((3,)),
            dma((3,)), dma((3,)),
            dma((3, 2, 6)), dma((3, 2, 6)),
            dma((3, 12)), dma((3, 12)),
            dma((2, 2)), dma((2, 2)),
        ],
        compiler_params=pltpu.CompilerParams(
            collective_id=0, has_side_effects=True, vmem_limit_bytes=56 * 2**20
        ),
        cost_estimate=pl.CostEstimate(flops=8 * 10**9, bytes_accessed=4 * 10**6, transcendentals=0),
    )(three_index[0], occ_energy, vir_energy[None, :])
    return gamma[None, :v]


def solution(mesh):
    placed = (P("occ", None, "aux"), P(), P())
    return jax.shard_map(
        functools.partial(local, mesh.shape["occ"]),
        mesh=mesh, in_specs=placed, out_specs=P("occ", None, "aux"), check_vma=False,
    )
```

```python
import functools

import jax
import jax.numpy as jnp
from jax import lax
from jax.experimental import pallas as pl
from jax.experimental.pallas import tpu as pltpu
from jax.sharding import PartitionSpec as P

MESH = pl.DeviceIdType.MESH
PAD = 1024
BLOCK = 128
HALF = 512
SPLITS = ((512, 512), (512, 512), (512, 640))
SELF_COLS = 640
SELF_NEAR = 384
F32 = jnp.float32
BF16 = jnp.bfloat16


def kernel(
    n_occ, b_in, occ_ref, vir_ref, g_ref,
    b_ref, vrow, vwrap, quad, vcol, bp, nbo, nbp, kf, kp, kr, kx, km, am, ret, rchip, rz,
    x_ss, x_rs, z_ss, z_rs, c_ss, c_rs, k_ss, k_rs, a_ss, a_rs, r_ss, r_rs,
):
    occ = lax.axis_index("occ")
    aux = lax.axis_index("aux")
    core = lax.rem(occ, 2)
    y = lax.div(aux, 2)
    h = lax.rem(aux, 2)
    o = 1 - h
    z = lax.rem(lax.div(occ, 2), 8)
    crowded = z * (7 - z) == 0
    yp, ym, yy = lax.rem(y + 1, 4), lax.rem(y + 3, 4), lax.rem(y + 2, 4)

    def orbital(d):
        return lax.rem(occ + d + n_occ, n_occ)

    across = (occ, y * 2 + o)
    up, down, far = [(occ, q * 2 + h) for q in (yp, ym, yy)]
    sibling = (occ + 1 - 2 * core, aux)
    z_out = (orbital(4 * core - 2), aux)
    z_in = (orbital(2 - 4 * core), aux)
    zs, cs = 1 - core, core
    e_mine = occ_ref[occ]
    e_pair = (e_mine, occ_ref[orbital(-1 - core)], occ_ref[orbital(2 - 3 * core)])

    barrier = pltpu.get_barrier_semaphore()
    greeted = (across, up, down, far, sibling, z_out, z_in)
    for dev in greeted:
        pl.semaphore_signal(barrier, inc=1, device_id=dev, device_id_type=MESH)

    v = b_in.shape[0]
    whole = v // 16 * 16
    b_ref[:whole, :] = b_in[:whole, :]
    tail = jnp.zeros((PAD - v, b_in.shape[1]), F32)
    b_ref[whole:, :] = jnp.concatenate([b_in[whole:, :].astype(F32), tail], axis=0).astype(BF16)
    vrow[...] = jnp.ones_like(vrow)
    vrow[:, :v] = vir_ref[...]
    for n in range(2):
        vwrap[:, n * HALF:(n + 1) * HALF] = vrow[:, pl.ds(pl.multiple_of(h * HALF, HALF), HALF)]
    base = pl.multiple_of(h * HALF + y * BLOCK, BLOCK)
    here = jnp.broadcast_to(vrow[:, pl.ds(base, BLOCK)], (BLOCK, BLOCK))
    diagonal = lax.broadcasted_iota(jnp.int32, (BLOCK, BLOCK), 0) == lax.broadcasted_iota(jnp.int32, (BLOCK, BLOCK), 1)
    vcol[...] = jnp.sum(jnp.where(diagonal, here, 0.0), axis=1, keepdims=True)
    pl.semaphore_wait(barrier, len(greeted))

    def remote(src, dst, ss, rs, dev):
        return pltpu.make_async_remote_copy(
            src_ref=src, dst_ref=dst, send_sem=ss, recv_sem=rs, device_id=dev, device_id_type=MESH
        )

    sent = []

    def push(*args):
        c = remote(*args)
        c.start()
        sent.append(c)

    def ds(start, size):
        return pl.ds(pl.multiple_of(start, size), size)

    rows_h, rows_o = ds(h * HALF, HALF), ds(o * HALF, HALF)

    push(b_ref.at[rows_o, :], bp.at[rows_o, :], x_ss.at[0], x_rs.at[0], across)

    def b_part(n, source):
        if source is None:
            return (b_ref.at[rows_h, :], bp.at[rows_h, :], b_ref.at[rows_o, :])[n]
        return (nbo.at[source, rows_h, :], nbp.at[source], nbo.at[source, rows_o, :])[n]

    def z_send(n):
        push(b_part(n, None), b_part(n, zs), z_ss.at[n], z_rs.at[n], z_out)

    def chip_send(n, source):
        remote(b_part(n, source), b_part(n, 1 - core), c_ss.at[n], c_rs.at[n], sibling).start()

    def z_arrive(n):
        remote(b_part(n, zs), b_part(n, zs), z_ss.at[n], z_rs.at[n], z_in).wait_recv()

    def chip_arrive(n):
        remote(b_part(n, cs), b_part(n, cs), c_ss.at[n], c_rs.at[n], sibling).wait_recv()

    def own_to_chip(n):
        @pl.when(core == 0)
        def _():
            chip_send(n, None)

    def slot_to_chip(n):
        z_arrive(n)

        @pl.when(core == 1)
        def _():
            chip_send(n, 0)

    def k_cols(k, ab):
        if k == 0:
            return pl.ds(SELF_NEAR, 256) if ab else pl.ds(0, SELF_NEAR)
        return ds((o if ab else h) * HALF, HALF)

    def half_rows(q, part):
        return ds(q * BLOCK + part * 64, 64)

    contract = (((1,), (1,)), ((), ()))

    def partial_k(k, ab):
        cols = k_cols(k, ab)
        if k == 0 and ab:
            for s in range(2):
                left = ds(h * HALF + s * 256, 256)
                right = ds(o * HALF + lax.rem(s + h, 2) * 256, 256)
                part = lax.dot_general(b_ref[left, :], b_ref[right, :], contract, preferred_element_type=F32)
                part += lax.dot_general(bp[left, :], bp[right, :], contract, preferred_element_type=F32)
                kf[k, pl.ds(s * 256, 256), cols] = part
                kp[k, pl.ds(s * 256, 256), cols] = part.astype(BF16)
        else:
            right = ds((o if ab else h) * HALF, HALF)
            left, left_p = (b_ref[rows_h, :], bp[rows_h, :]) if k == 0 else (nbo[k - 1, rows_h, :], nbp[k - 1])
            part = lax.dot_general(left, b_ref[right, :], contract, preferred_element_type=F32)
            part += lax.dot_general(left_p, bp[right, :], contract, preferred_element_type=F32)
            if k:
                kf[k, :, cols] = part
                kp[k, :, cols] = part.astype(BF16)
            else:
                for q in range(4):
                    for d in range(3):
                        r, c, at = q * BLOCK, (q + d) % 4 * BLOCK, d * BLOCK
                        block = part[r:r + BLOCK, c:c + BLOCK]
                        kf[0, r:r + BLOCK, at:at + BLOCK] = block
                        kp[0, r:r + BLOCK, at:at + BLOCK] = block.astype(BF16)
        push(kp.at[k, half_rows(yy, 0), cols], relayed(k, ab, 0), k_ss.at[k, ab, 0], k_rs.at[k, ab, 0], up)
        push(kp.at[k, half_rows(yy, 1), cols], relayed(k, ab, 1), k_ss.at[k, ab, 1], k_rs.at[k, ab, 1], down)
        push(kp.at[k, half_rows(yp, 1), cols], arrived(k, ab, 0, 1), k_ss.at[k, ab, 2], k_rs.at[k, ab, 2], up)
        push(kp.at[k, half_rows(ym, 0), cols], arrived(k, ab, 1, 0), k_ss.at[k, ab, 3], k_rs.at[k, ab, 3], down)

    def run(k, ab):
        return pl.ds(0, HALF if k else 256 if ab else SELF_NEAR)

    def relayed(k, ab, way):
        return kx.at[k, ab, way, :, run(k, ab)]

    def arrived(k, ab, way, part):
        return kr.at[k, way, pl.ds(part * 64, 64), k_cols(k, ab)]

    def pass_on(k, ab):
        for way, (source, target, q) in enumerate(((down, up, yp), (up, down, ym))):
            ref = relayed(k, ab, way)
            remote(ref, ref, k_rs.at[k, ab, way], k_rs.at[k, ab, way], source).wait_recv()
            width = run(k, ab)
            own = kf[k, half_rows(q, way), k_cols(k, ab)]
            km[k, ab, way, :, width] = (own + kx[k, ab, way, :, width].astype(F32)).astype(BF16)
            push(
                km.at[k, ab, way, :, width], arrived(k, ab, way, way),
                k_ss.at[k, ab, 4 + way], k_rs.at[k, ab, 4 + way], target,
            )

    def amplitude(k):
        for ab in range(2):
            cols = k_cols(k, ab)
            for n, (way, part) in ((2, (0, 1)), (3, (1, 0)), (4, (0, 0)), (5, (1, 1))):
                ref = arrived(k, ab, way, part)
                remote(ref, ref, k_rs.at[k, ab, n], k_rs.at[k, ab, n], up if way else down).wait_recv()
            source, energy = vrow, cols
            if k == 0 and ab:
                energy = ds(o * HALF + lax.rem(y // 2 + h, 2) * 256, 256)
            elif k == 0:
                source, energy = vwrap, pl.ds(pl.multiple_of(y * BLOCK, BLOCK), SELF_NEAR)

            @pl.loop(0, 4)
            def _(t):
                total = kf[k, ds(y * BLOCK + t * 32, 32), cols]
                for way in range(2):
                    total += kr[k, way, ds(t * 32, 32), cols].astype(F32)
                denom = vcol[ds(t * 32, 32), :] + source[:, energy] - e_mine - e_pair[k]
                am[k, ds(base + t * 32, 32), cols] = (total / denom).astype(BF16)

    def piece(k, n, side, q, low, w):
        count = 64 if n in (2, 3, 7, 8) else BLOCK
        width = PAD if k else SELF_COLS
        split = SPLITS[k][w]
        cols = pl.ds(0, width) if n < 5 else pl.ds(0, split) if n < 9 else pl.ds(split, width - split)
        return am.at[k, ds(side * HALF + q * BLOCK + low, count), cols]

    def by_plane(f):
        pl.when(crowded)(lambda: f(1))
        pl.when(jnp.logical_not(crowded))(lambda: f(0))

    def spread(k, n, side, q, low, dev, w=0):
        ref = piece(k, n, side, q, low, w)
        remote(ref, ref, a_ss.at[k, n], a_rs.at[k, n], dev).start()

    def gather_from(k, n, w=0):
        q, low = ((ym, 0), (yp, 0), (yy, 0), (yy, 64), (y, 0), (ym, 0), (yp, 0), (yy, 0), (yy, 64), (ym, 0), (yp, 0), (yy, 0))[n]
        dev = (down, up, down, up, across, down, up, down, up, across, across, across)[n]
        ref = piece(k, n, h if n < 4 else o, q, low, w)
        remote(ref, ref, a_ss.at[k, n], a_rs.at[k, n], dev).wait_recv()

    def stage1(k):
        spread(k, 4, h, y, 0, across)
        spread(k, 0, h, y, 0, up)
        spread(k, 1, h, y, 0, down)

    def stage2(k):
        @by_plane
        def _(w):
            gather_from(k, 0)
            spread(k, 2, h, ym, 0, up)
            spread(k, 9, h, ym, 0, across, w)
            gather_from(k, 1)
            spread(k, 3, h, yp, 64, down)
            spread(k, 10, h, yp, 0, across, w)
            gather_from(k, 4)
            spread(k, 5, o, y, 0, up, w)
            spread(k, 6, o, y, 0, down, w)

    def stage3(k):
        @by_plane
        def _(w):
            gather_from(k, 2)
            gather_from(k, 3)
            spread(k, 11, h, yy, 0, across, w)
            gather_from(k, 5, w)
            spread(k, 7, o, ym, 0, up, w)
            gather_from(k, 6, w)
            spread(k, 8, o, yp, 64, down, w)

    def stage4(k):
        @by_plane
        def _(w):
            for n in (7, 8, 9, 10, 11):
                gather_from(k, n, w)

    def product(k, transposed, right, store):
        @pl.loop(0, 2)
        def _(t):
            r = ds(t * HALF, HALF)
            if transposed:
                term = lax.dot_general(am[k, :, r], right, (((0,), (0,)), ((), ())), preferred_element_type=F32)
            else:
                term = jnp.dot(am[k, r, :], right, preferred_element_type=F32)
            store(r, term)

    def set_gamma(r, term):
        g_ref[r, :] = term

    def add_gamma(r, term):
        g_ref[r, :] += term

    def set_return(n):
        def store(r, term):
            ret[n, r, :] = term.astype(BF16)

        return store

    def self_product(side):
        for q in range(4):
            r, last = q * BLOCK, (q + 3) % 4 * BLOCK
            for d in range(3):
                c = (q + d) % 4 * BLOCK
                quad[r:r + BLOCK, c:c + BLOCK] = am[0, ds(side * HALF + r, BLOCK), pl.ds(d * BLOCK, BLOCK)]
            quad[r:r + BLOCK, last:last + BLOCK] = am[0, ds(side * HALF + last, BLOCK), pl.ds(BLOCK, BLOCK)].T
        r = ds(side * HALF, HALF)
        g_ref[r, :] += jnp.dot(quad[...], b_ref[r, :], preferred_element_type=F32)
        for s in range(2):
            r = ds(side * HALF + s * 256, 256)
            c = ds((1 - side) * HALF + lax.rem(s + side, 2) * 256, 256)
            block = am[0, r, pl.ds(SELF_NEAR, 256)]
            g_ref[r, :] += jnp.dot(block, b_ref[c, :], preferred_element_type=F32)
            g_ref[c, :] += lax.dot_general(block, b_ref[r, :], (((0,), (0,)), ((), ())), preferred_element_type=F32)

    def return_part(n, half, dst, dev):
        rows = rows_o if half else rows_h
        m = 0 if dst is rchip else 1
        return remote(ret.at[n, rows, :], dst.at[rows, :], r_ss.at[m, half], r_rs.at[m, half], dev)

    def give_back(k, half):
        rows = rows_o if half else rows_h
        ret[k - 1, rows, :] = jnp.dot(am[k, rows, :], b_ref[...], preferred_element_type=F32).astype(BF16)

        @pl.when(core == k - 1)
        def _():
            return_part(k - 1, half, rchip, sibling).start()

        if k == 2:
            @pl.when(core == 0)
            def _():
                return_part(1, half, rz, z_in).start()

    def merge(half):
        rows = rows_o if half else rows_h

        @pl.when(core == 1)
        def _():
            return_part(0, half, rchip, sibling).wait_recv()
            ret[0, rows, :] = (ret[0, rows, :].astype(F32) + rchip[rows, :].astype(F32)).astype(BF16)
            return_part(0, half, rz, z_in).start()

    z_send(0)
    push(b_ref.at[rows_h, :], bp.at[rows_h, :], x_ss.at[1], x_rs.at[1], across)
    own_to_chip(0)
    slot_to_chip(0)
    remote(bp.at[rows_h, :], bp.at[rows_h, :], x_ss.at[0], x_rs.at[0], across).wait_recv()
    z_send(1)
    own_to_chip(1)
    partial_k(0, 0)
    slot_to_chip(1)
    chip_arrive(0)
    chip_arrive(1)
    partial_k(2, 0)
    pass_on(0, 0)
    partial_k(1, 0)
    pass_on(2, 0)
    remote(bp.at[rows_o, :], bp.at[rows_o, :], x_ss.at[1], x_rs.at[1], across).wait_recv()
    z_send(2)
    own_to_chip(2)
    partial_k(1, 1)
    pass_on(1, 0)
    partial_k(2, 1)
    pass_on(1, 1)
    partial_k(0, 1)
    pass_on(2, 1)
    amplitude(1)
    stage1(1)
    pass_on(0, 1)
    slot_to_chip(2)
    amplitude(2)
    stage1(2)
    stage2(1)
    amplitude(0)
    stage1(0)
    stage2(2)
    stage3(1)
    give_back(1, 0)
    merge(0)
    stage3(2)
    give_back(2, 0)
    stage2(0)
    chip_arrive(2)
    stage4(1)
    give_back(1, 1)
    product(1, True, nbo[0], set_gamma)
    merge(1)
    stage3(0)
    stage4(2)
    give_back(2, 1)
    product(2, True, nbo[1], add_gamma)
    self_product(h)
    stage4(0)
    self_product(o)
    for half in range(2):
        return_part(1, half, rz, z_out).wait_recv()

    @pl.loop(0, 8)
    def _(t):
        r = ds(t * BLOCK, BLOCK)
        g_ref[r, :] += rz[r, :].astype(F32)

    @pl.when(core == 0)
    def _():
        for half in range(2):
            return_part(1, half, rchip, sibling).wait_recv()

        @pl.loop(0, 8)
        def _(t):
            r = ds(t * BLOCK, BLOCK)
            g_ref[r, :] += rchip[r, :].astype(F32)

    for c in sent:
        c.wait_send()

    @by_plane
    def _(w):
        for k in range(3):
            for n in range(12):
                ref = piece(k, n, 0, 0, 0, w)
                remote(ref, ref, a_ss.at[k, n], a_rs.at[k, n], across).wait_send()

    for n in range(3):
        remote(b_part(n, cs), b_part(n, cs), c_ss.at[n], c_rs.at[n], sibling).wait_send()
    for half in range(2):
        return_part(0, half, rchip, sibling).wait_send()
        return_part(0, half, rz, z_in).wait_send()


def local(n_occ, three_index, occ_energy, vir_energy):
    v = three_index.shape[1]
    width = three_index.shape[2]
    vmem = pl.BlockSpec(memory_space=pltpu.VMEM)
    dma = pltpu.SemaphoreType.DMA
    gamma = pl.pallas_call(
        functools.partial(kernel, n_occ),
        out_shape=jax.ShapeDtypeStruct((PAD, width), F32),
        in_specs=[vmem, pl.BlockSpec(memory_space=pltpu.SMEM), vmem],
        out_specs=vmem,
        scratch_shapes=[
            pltpu.VMEM((PAD, width), BF16),
            pltpu.VMEM((1, PAD), F32),
            pltpu.VMEM((1, PAD), F32),
            pltpu.VMEM((HALF, HALF), BF16),
            pltpu.VMEM((BLOCK, 1), F32),
            pltpu.VMEM((PAD, width), BF16),
            pltpu.VMEM((2, PAD, width), BF16),
            pltpu.VMEM((2, HALF, width), BF16),
            pltpu.VMEM((3, HALF, PAD), F32),
            pltpu.VMEM((3, HALF, PAD), BF16),
            pltpu.VMEM((3, 2, BLOCK, PAD), BF16),
            pltpu.VMEM((3, 2, 2, 64, HALF), BF16),
            pltpu.VMEM((3, 2, 2, 64, HALF), BF16),
            pltpu.VMEM((3, PAD, PAD), BF16),
            pltpu.VMEM((2, PAD, width), BF16),
            pltpu.VMEM((PAD, width), BF16),
            pltpu.VMEM((PAD, width), BF16),
            dma((2,)), dma((2,)),
            dma((3,)), dma((3,)),
            dma((3,)), dma((3,)),
            dma((3, 2, 6)), dma((3, 2, 6)),
            dma((3, 12)), dma((3, 12)),
            dma((2, 2)), dma((2, 2)),
        ],
        compiler_params=pltpu.CompilerParams(
            collective_id=0, has_side_effects=True, vmem_limit_bytes=56 * 2**20
        ),
        cost_estimate=pl.CostEstimate(flops=8 * 10**9, bytes_accessed=4 * 10**6, transcendentals=0),
    )(three_index[0], occ_energy, vir_energy[None, :])
    return gamma[None, :v]


def solution(mesh):
    placed = (P("occ", None, "aux"), P(), P())
    return jax.shard_map(
        functools.partial(local, mesh.shape["occ"]),
        mesh=mesh, in_specs=placed, out_specs=P("occ", None, "aux"), check_vma=False,
    )
```
